32 devices in a mesh: wide: 16 (over z, y, x), narrow: 2 (over core).
Axes of the slice: x: 2, y: 2, z: 4, core: 2. Of those that a mesh axis runs over, the one named last changes fastest.
Arguments:
- integrals: bfloat16 [4096, 65536], P('wide', 'narrow'), may hold values from -0.03125 to 0.03125
- amp_tiles: bfloat16 [2, 3145728], P('narrow', 'wide'), may hold values from -6 to 6
- row_orbitals: int32 [4096, 2], P('wide'), may hold values from 0 to 511
- orb_irrep: int32 [512], replicated, may hold values from 0 to 3
- occ_pairs: int32 [96, 2], replicated, may hold values from 0 to 15
- occ_irrep: int32 [16], replicated, may hold values from 0 to 3
Outputs:
- residual: float32 [4096, 96], P(('wide', 'narrow'))
The draws below stay inside these ranges and needn't reach their ends.
All inputs are finite; a program needn't handle non-finite values.
Results may differ from the reference program's by a relative error of at most 0.0003.
Values may be sent and summed in bfloat16 or wider, within the bound.
No kernel may reach another device: no remote copies, remote signals or barrier semaphores. Data moves between devices by JAX's collectives and lax.ppermute only.
A program may use at most 64 MiB of HBM per device.

```python
import jax
import jax.numpy as jnp

NV = 512
NIRREP = 4
NOCC = 16
NPAIR = 96
COLS = 65536
ROWS = 4096
COL_DEV = 32768
N_NARROW = 2


def place_ends(result, stream_key, least, top_value):
    place = [jax.random.randint(jax.random.fold_in(stream_key, axis), (), 0, length) for axis, length in enumerate(result.shape)]
    longest = result.shape.index(max(result.shape))
    next_to = place[:longest] + [(place[longest] + 1) % result.shape[longest]] + place[longest + 1:]
    return result.at[tuple(place)].set(least).at[tuple(next_to)].set(top_value)


def strengthened(array, own_key, source, target, shards_of, factor):
    owner, partner = [(jnp.arange(array.shape[axis_at]) // (array.shape[axis_at] // shards_of)).reshape([-1 if axis == axis_at else 1 for axis in range(array.ndim)]) for axis_at in (source, target)]
    chosen = jax.random.permutation(own_key, shards_of)[partner]
    strong = (owner == chosen) | (owner == (partner + shards_of // 2) % shards_of)
    return jnp.where(strong, factor * array, array)


def shard_levels(key, extent, cuts, smallest, largest):
    def one(axis_at, shards_of):
        heights = jax.random.uniform(jax.random.fold_in(jax.random.fold_in(key, 6), axis_at), (shards_of,), jnp.float32, smallest / len(cuts), largest / len(cuts))
        return jnp.repeat(jnp.exp(heights), extent[axis_at] // shards_of).reshape((-1,) + (1,) * (len(extent) - axis_at - 1))

    level = one(*cuts[0])
    for cut in cuts[1:]:
        level = level * one(*cut)
    return level


def centred(key, extent, deviation, limit, pieces=(), held_as=jnp.bfloat16):
    values = deviation * jax.random.normal(key, extent, jnp.float32)
    if pieces:
        values = values * shard_levels(key, extent, pieces, -0.22, 0.18)
    return jnp.clip(values, -limit, limit).astype(held_as)


def bell_draw_with(own_key, shape, scale, reach, pieces, heavy, dtype=jnp.bfloat16):
    drawn = scale * jax.random.normal(own_key, shape, jnp.float32)
    if pieces:
        drawn = drawn * shard_levels(own_key, shape, pieces, -0.22, 0.18)
    return jnp.clip(strengthened(drawn, jax.random.fold_in(own_key, 3), *heavy), -reach, reach).astype(dtype)


def setup_inputs(seed: int = 0) -> dict:
    streams_of = jax.random.split(jax.random.key(seed), 7)
    return {
        "integrals": bell_draw_with(streams_of[0], (ROWS, COLS), COLS ** -0.5, 0.03125, ((0, 16), (1, 2)), (1, 0, 16, 2.0)),
        "amp_tiles": centred(streams_of[1], (N_NARROW, COL_DEV * NPAIR), 1.0, 6.0, ((0, 2), (1, 16))),
        "row_orbitals": place_ends(jax.random.randint(streams_of[2], (ROWS, 2), 0, NV), jax.random.fold_in(streams_of[2], 1), 0, NV - 1).astype(jnp.int32),
        "orb_irrep": place_ends(jax.random.randint(streams_of[3], (NV,), 0, NIRREP), jax.random.fold_in(streams_of[3], 1), 0, NIRREP - 1).astype(jnp.int32),
        "occ_pairs": place_ends(jax.random.randint(streams_of[4], (NPAIR, 2), 0, NOCC), jax.random.fold_in(streams_of[4], 1), 0, NOCC - 1).astype(jnp.int32),
        "occ_irrep": place_ends(jax.random.randint(streams_of[5], (NOCC,), 0, NIRREP), jax.random.fold_in(streams_of[5], 1), 0, NIRREP - 1).astype(jnp.int32),
    }


def reference(integrals, amp_tiles, row_orbitals, orb_irrep, occ_pairs, occ_irrep):
    amplitudes = amp_tiles.reshape(COLS, NPAIR)
    ladder = jnp.dot(integrals, amplitudes, preferred_element_type=jnp.float32)
    row_sym = jnp.bitwise_xor(orb_irrep[row_orbitals[:, 0]], orb_irrep[row_orbitals[:, 1]])
    pair_sym = jnp.bitwise_xor(occ_irrep[occ_pairs[:, 0]], occ_irrep[occ_pairs[:, 1]])
    keep = row_sym[:, None] == pair_sym[None, :]
    return jnp.where(keep, ladder, jnp.zeros_like(ladder))
```

```python
import functools

import jax
import jax.numpy as jnp
from jax import lax
from jax.experimental import pallas as pl
from jax.experimental.pallas import tpu as pltpu
from jax.sharding import PartitionSpec as P

LANES = 128
X, Y, Z1, Z2 = 1, 2, 4, 8
STEPS = (
    ("A", Z1, "O"), ("XO", X, "O"), ("YO", Y, "O"), ("B", Z2, "O"),
    ("DO", X, "YO"), ("YA", Y, "A"), ("C", Z1, "B"), ("XB", X, "B"), ("YB", Y, "B"),
    ("DA", Z1, "DO"), ("XA", X, "A"), ("DB", Y, "XB"), ("YC", Y, "C"), ("XC", X, "C"),
    ("DC", Z1, "DB"),
)
GROUPS = (("O",), ("A", "XO", "YO", "B"), ("DO", "YA", "C"), ("XB", "YB", "DA"), ("XA", "DB", "YC"), ("XC", "DC"))


def lookup_irrep(orbitals, table):
    hits = orbitals[..., None] == jnp.arange(table.shape[0], dtype=jnp.int32)
    return jnp.sum(jnp.where(hits, table, 0), axis=-1)


def transpose_kernel(pairs, tile_ref, out_ref, flat, rows):
    depth = flat.shape[0] // 3
    flat[...] = tile_ref[...].astype(jnp.float32).reshape(flat.shape)
    x0, x1, x2 = [flat[pl.ds(s, depth, stride=3), :] for s in range(3)]
    lane = lax.broadcasted_iota(jnp.int32, x0.shape, 1)
    rows[pl.ds(0, depth, stride=4), :] = x0
    rows[pl.ds(1, depth, stride=4), :] = jnp.where(lane < 32, pltpu.roll(x0, 32, 1), pltpu.roll(x1, 32, 1))
    rows[pl.ds(2, depth, stride=4), :] = jnp.where(lane < 64, pltpu.roll(x1, 64, 1), pltpu.roll(x2, 64, 1))
    rows[pl.ds(3, depth, stride=4), :] = pltpu.roll(x2, 96, 1)
    out_ref[...] = rows[...].T[:pairs].astype(out_ref.dtype)


def transposed_tile(tile, pairs):
    size = tile.shape[1]
    return pl.pallas_call(
        functools.partial(transpose_kernel, pairs),
        out_shape=jax.ShapeDtypeStruct((pairs, size // pairs), tile.dtype),
        scratch_shapes=[
            pltpu.VMEM((size // LANES, LANES), jnp.float32),
            pltpu.VMEM((size // pairs, LANES), jnp.float32),
        ],
        name="transpose_tile",
    )(tile)


def product(left, right):
    return lax.dot_general(left, right, (((1,), (1,)), ((), ())), preferred_element_type=jnp.float32)


def group_kernel(count, has_total, columns_ref, integrals_ref, *refs):
    chunks, out_ref = refs[:count], refs[-1]
    step = pl.program_id(0)

    @pl.when(step == 0)
    def _():
        out_ref[...] = refs[count][...] if has_total else jnp.zeros_like(out_ref)

    for k in range(count):
        @pl.when(step == k)
        def _():
            out_ref[...] += product(integrals_ref[...], chunks[k][...])


def add_group(integrals, chunks, columns, total):
    rows = integrals.shape[0]
    pairs, depth = chunks[0].shape
    whole = lambda shape: pl.BlockSpec(shape, lambda i, c: (0, 0))
    extra = [] if total is None else [total]
    return pl.pallas_call(
        functools.partial(group_kernel, len(chunks), total is not None),
        out_shape=jax.ShapeDtypeStruct((rows, pairs), jnp.float32),
        grid_spec=pltpu.PrefetchScalarGridSpec(
            num_scalar_prefetch=1,
            grid=(len(chunks),),
            in_specs=[pl.BlockSpec((rows, depth), lambda i, c: (0, c[i]))]
            + [whole((pairs, depth))] * len(chunks) + [whole((rows, pairs))] * len(extra),
            out_specs=whole((rows, pairs)),
        ),
        cost_estimate=pl.CostEstimate(
            flops=2 * rows * depth * pairs * len(chunks), bytes_accessed=2 * rows * depth * len(chunks), transcendentals=0
        ),
        compiler_params=pltpu.CompilerParams(vmem_limit_bytes=16 * 2**20),
        name="add_group",
    )(columns, integrals, *chunks, *extra)


def ring_kernel(integrals_ref, chunk_ref, out_ref):
    @pl.when(pl.program_id(0) == 0)
    def _():
        out_ref[...] = jnp.zeros_like(out_ref)

    out_ref[...] += product(integrals_ref[...], chunk_ref[0])


def gathered_product(integrals, own, axis_size):
    rows, (pairs, depth) = integrals.shape[0], own.shape
    gathered = lax.all_gather(own, "wide", axis=0)
    return pl.pallas_call(
        ring_kernel,
        out_shape=jax.ShapeDtypeStruct((rows, pairs), jnp.float32),
        grid=(axis_size,),
        in_specs=[
            pl.BlockSpec((rows, depth), lambda i: (0, i)),
            pl.BlockSpec((1, pairs, depth), lambda i: (i, 0, 0)),
        ],
        out_specs=pl.BlockSpec((rows, pairs), lambda i: (0, 0)),
        name="gathered_product",
    )(integrals, gathered)


def exchanged_product(integrals, own):
    me = lax.axis_index("wide")
    held, distance = {"O": own}, {"O": 0}
    for name, step, source in STEPS:
        held[name] = lax.ppermute(held[source], "wide", [(i, i ^ step) for i in range(16)])
        distance[name] = distance[source] ^ step
    total = None
    for group in GROUPS:
        columns = jnp.stack([me ^ distance[name] for name in group]).astype(jnp.int32)
        total = add_group(integrals, [held[name] for name in group], columns, total)
    return total


def shards(wide, narrow, integrals, amp_tiles, row_orbitals, orb_irrep, occ_pairs, occ_irrep):
    pairs = occ_pairs.shape[0]
    part = integrals.shape[0] // narrow
    row_labels = lookup_irrep(row_orbitals, orb_irrep)
    pair_labels = lookup_irrep(occ_pairs, occ_irrep)
    row_sym = jnp.bitwise_xor(row_labels[:, 0], row_labels[:, 1])
    pair_sym = jnp.bitwise_xor(pair_labels[:, 0], pair_labels[:, 1])
    own = transposed_tile(amp_tiles, pairs)
    if (wide, narrow) != (16, 2):
        block = gathered_product(integrals, own, wide)
        block = jnp.where(row_sym[:, None] == pair_sym[None, :], block, jnp.zeros_like(block))
        return lax.psum_scatter(block, "narrow", scatter_dimension=0, tiled=True)
    total = exchanged_product(integrals, own)
    core = lax.axis_index("narrow")
    mine = lax.dynamic_slice_in_dim(total, core * part, part, 0)
    other = lax.dynamic_slice_in_dim(total, (1 - core) * part, part, 0)
    sym = lax.dynamic_slice_in_dim(row_sym, core * part, part, 0)
    summed = mine + lax.ppermute(other, "narrow", [(0, 1), (1, 0)])
    return jnp.where(sym[:, None] == pair_sym[None, :], summed, jnp.zeros_like(summed))


def solution(mesh):
    in_specs = (P("wide", "narrow"), P("narrow", "wide"), P("wide", None), P(), P(), P())
    out_specs = P(("wide", "narrow"), None)
    body = functools.partial(shards, mesh.shape["wide"], mesh.shape["narrow"])
    return jax.shard_map(body, mesh=mesh, in_specs=in_specs, out_specs=out_specs, check_vma=False)
```

```python
import functools

import jax
import jax.numpy as jnp
from jax import lax
from jax.experimental import pallas as pl
from jax.experimental.pallas import tpu as pltpu
from jax.sharding import PartitionSpec as P

LANES = 128
MIB = 2**20
X, Y, Z1, Z2, Z3 = 1, 2, 4, 8, 12
LOAD, MULTIPLY, STEP = "load", "multiply", "step"
EVENTS = (
    ("A", Z1, "O"), ("YO", Y, "O"), ("XO", X, "O"), LOAD, ("C", Z3, "O"), ("A",), ("YA", Y, "A"), STEP, ("YO",), STEP,
    ("XO",), ("DO", Y, "XO"), ("XA", X, "A"), LOAD, MULTIPLY, ("C",), ("XC", X, "C"), ("YC", Y, "C"), STEP, ("YA",),
    ("YB", Z3, "YA"), STEP, ("DO",), ("B", Z1, "C"), MULTIPLY, ("XA",), ("DA", X, "YA"), STEP, ("XC",),
    ("DC", Y, "XC"), STEP, ("YC",), ("XB", Z1, "XC"), MULTIPLY, ("YB",), ("DB", X, "YB"), STEP, ("B",), STEP, ("DA",),
    MULTIPLY, ("DC",), STEP, ("XB",), STEP, ("DB",),
)
LOADS = (2, None)
COST = pl.CostEstimate(flops=1, bytes_accessed=4 * 10**6, transcendentals=0)
ANYWHERE = pl.BlockSpec(memory_space=pl.ANY)
VMEM = pl.BlockSpec(memory_space=pltpu.VMEM)


def lookup_irrep(orbitals, table):
    hits = orbitals[..., None] == jnp.arange(table.shape[0], dtype=jnp.int32)
    return jnp.sum(jnp.where(hits, table, 0), axis=-1)


def transpose_kernel(pairs, tile_ref, out_ref, flat, rows):
    depth = flat.shape[0] // 3
    flat[...] = tile_ref[...].astype(jnp.float32).reshape(flat.shape)
    x0, x1, x2 = [flat[pl.ds(s, depth, stride=3), :] for s in range(3)]
    lane = lax.broadcasted_iota(jnp.int32, x0.shape, 1)
    rows[pl.ds(0, depth, stride=4), :] = x0
    rows[pl.ds(1, depth, stride=4), :] = jnp.where(lane < 32, pltpu.roll(x0, 32, 1), pltpu.roll(x1, 32, 1))
    rows[pl.ds(2, depth, stride=4), :] = jnp.where(lane < 64, pltpu.roll(x1, 64, 1), pltpu.roll(x2, 64, 1))
    rows[pl.ds(3, depth, stride=4), :] = pltpu.roll(x2, 96, 1)
    out_ref[...] = rows[...].T[:pairs].astype(out_ref.dtype)


def transposed_tile(tile, pairs):
    size = tile.shape[1]
    return pl.pallas_call(
        functools.partial(transpose_kernel, pairs),
        out_shape=jax.ShapeDtypeStruct((pairs, size // pairs), tile.dtype),
        scratch_shapes=[
            pltpu.VMEM((size // LANES, LANES), jnp.float32),
            pltpu.VMEM((size // pairs, LANES), jnp.float32),
        ],
        compiler_params=pltpu.CompilerParams(vmem_limit_bytes=8 * MIB),
        name="transpose_tile",
    )(tile)


def product(left, right):
    return lax.dot_general(left, right, (((1,), (1,)), ((), ())), preferred_element_type=jnp.float32)


def step_kernel(mark_ref, out_ref):
    pass


def mark_step(mark):
    return pl.pallas_call(
        step_kernel,
        out_shape=jax.ShapeDtypeStruct(mark.shape, mark.dtype),
        in_specs=[ANYWHERE],
        out_specs=ANYWHERE,
        input_output_aliases={0: 0},
        cost_estimate=COST,
        compiler_params=pltpu.CompilerParams(vmem_limit_bytes=MIB),
        name="mark_step",
    )(mark)


def load_kernel(depth, distances, integrals_ref, mark_ref, loaded_ref, mark_out_ref, sems):
    me = lax.axis_index("wide")
    copies = []
    for k, distance in enumerate(distances):
        column = pl.multiple_of((me ^ distance) * depth, depth)
        source = integrals_ref.at[:, pl.ds(column, depth)]
        copies.append(pltpu.make_async_copy(source, loaded_ref.at[:, pl.ds(k * depth, depth)], sems.at[k]))
    for copy in copies:
        copy.start()
    for copy in copies:
        copy.wait()


def load_columns(integrals, mark, depth, distances):
    return pl.pallas_call(
        functools.partial(load_kernel, depth, distances),
        out_shape=[
            jax.ShapeDtypeStruct((integrals.shape[0], depth * len(distances)), integrals.dtype),
            jax.ShapeDtypeStruct(mark.shape, mark.dtype),
        ],
        in_specs=[ANYWHERE, ANYWHERE],
        out_specs=[VMEM, ANYWHERE],
        input_output_aliases={1: 1},
        scratch_shapes=[pltpu.SemaphoreType.DMA((len(distances),))],
        cost_estimate=COST,
        compiler_params=pltpu.CompilerParams(vmem_limit_bytes=40 * MIB),
        name="load_columns",
    )(integrals, mark)


def multiply_kernel(first, count, last, mark_ref, loaded_ref, *refs):
    chunks, sum_ref = refs[:count], refs[-2]
    depth = chunks[0].shape[1]
    sums = refs[count][...] if len(refs) > count + 2 else None
    for k, chunk in enumerate(chunks):
        term = product(loaded_ref[:, pl.ds((first + k) * depth, depth)], chunk[...])
        sums = term if sums is None else sums + term
    sum_ref[...] = sums.T if last else sums


def multiply_chunks(mark, loaded, first, chunks, total, last):
    rows, pairs = loaded.shape[0], chunks[0].shape[0]
    operands = [loaded, *chunks] + ([] if total is None else [total])
    return pl.pallas_call(
        functools.partial(multiply_kernel, first, len(chunks), last),
        out_shape=[
            jax.ShapeDtypeStruct((pairs, rows) if last else (rows, pairs), jnp.float32),
            jax.ShapeDtypeStruct(mark.shape, mark.dtype),
        ],
        in_specs=[ANYWHERE] + [VMEM] * len(operands),
        out_specs=[VMEM, ANYWHERE],
        input_output_aliases={0: 1},
        cost_estimate=COST,
        compiler_params=pltpu.CompilerParams(vmem_limit_bytes=24 * MIB),
        name="multiply_chunks",
    )(mark, *operands)


def ring_kernel(integrals_ref, chunk_ref, out_ref):
    @pl.when(pl.program_id(0) == 0)
    def _():
        out_ref[...] = jnp.zeros_like(out_ref)

    out_ref[...] += product(integrals_ref[...], chunk_ref[0])


def gathered_product(integrals, own, axis_size):
    rows, (pairs, depth) = integrals.shape[0], own.shape
    gathered = lax.all_gather(own, "wide", axis=0)
    return pl.pallas_call(
        ring_kernel,
        out_shape=jax.ShapeDtypeStruct((rows, pairs), jnp.float32),
        grid=(axis_size,),
        in_specs=[
            pl.BlockSpec((rows, depth), lambda i: (0, i)),
            pl.BlockSpec((1, pairs, depth), lambda i: (i, 0, 0)),
        ],
        out_specs=pl.BlockSpec((rows, pairs), lambda i: (0, 0)),
        name="gathered_product",
    )(integrals, gathered)


def plan_of_events():
    distance, groups, arrived = {"O": 0}, [], ["O"]
    for event in EVENTS:
        if event == MULTIPLY:
            groups.append(arrived)
            arrived = []
        elif len(event) == 3:
            name, step, source = event
            distance[name] = distance[source] ^ step
        elif len(event) == 1:
            arrived.append(event[0])
    groups.append(arrived)
    assert sorted(distance[name] for names in groups for name in names) == list(range(16))
    return distance, groups


def exchanged_product(integrals, own, labels):
    depth = own.shape[1]
    distance, groups = plan_of_events()
    held, seen, total = {"O": own}, [], None
    mark = jnp.zeros((8, LANES), jnp.float32)
    loaded, loads, multiplied = {}, 0, 0

    def after(value, *earlier):
        return lax.optimization_barrier((value, mark, *[held[name] for name in seen], *earlier))

    def multiply():
        ready = after(mark)[0]
        names = groups[multiplied]
        array, first = loaded[multiplied]
        last = multiplied == len(groups) - 1
        return multiply_chunks(ready, array, first, [held[name] for name in names], total, last)

    for event in EVENTS:
        if event == STEP:
            mark = mark_step(after(mark)[0])
        elif event == LOAD:
            ready = after(mark, *(labels if loads else ()))[0]
            begin = LOADS[loads - 1] if loads else 0
            chosen = list(range(len(groups)))[begin:LOADS[loads]]
            names = [name for k in chosen for name in groups[k]]
            array, mark = load_columns(integrals, ready, depth, tuple(distance[name] for name in names))
            for k in chosen:
                loaded[k] = (array, names.index(groups[k][0]))
            loads += 1
        elif event == MULTIPLY:
            total, mark = multiply()
            multiplied += 1
        elif len(event) == 3:
            name, step, source = event
            value, mark, *_ = after(held[source], *([] if total is None else [total]))
            held[name] = lax.ppermute(value, "wide", [(i, i ^ step) for i in range(16)])
        else:
            seen.append(event[0])
    return multiply()[0]


def shards(wide, narrow, integrals, amp_tiles, row_orbitals, orb_irrep, occ_pairs, occ_irrep):
    pairs = occ_pairs.shape[0]
    part = integrals.shape[0] // narrow
    row_labels = lookup_irrep(row_orbitals, orb_irrep)
    pair_labels = lookup_irrep(occ_pairs, occ_irrep)
    row_sym = jnp.bitwise_xor(row_labels[:, 0], row_labels[:, 1])
    pair_sym = jnp.bitwise_xor(pair_labels[:, 0], pair_labels[:, 1])
    own = transposed_tile(amp_tiles, pairs)
    if (wide, narrow) != (16, 2):
        block = gathered_product(integrals, own, wide)
        block = jnp.where(row_sym[:, None] == pair_sym[None, :], block, jnp.zeros_like(block))
        return lax.psum_scatter(block, "narrow", scatter_dimension=0, tiled=True)
    core = lax.axis_index("narrow")
    row_sym = lax.dynamic_slice_in_dim(row_sym, core * part, part, 0)
    keep = (row_sym[None, :] == pair_sym[:, None]).astype(jnp.float32)
    total = exchanged_product(integrals, own, (keep,))
    mine = lax.dynamic_slice_in_dim(total, core * part, part, 1)
    other = lax.dynamic_slice_in_dim(total, (1 - core) * part, part, 1)
    summed = mine + lax.ppermute(other, "narrow", [(0, 1), (1, 0)])
    return jnp.where(keep > 0, summed, jnp.zeros_like(summed)).T


def solution(mesh):
    in_specs = (P("wide", "narrow"), P("narrow", "wide"), P("wide", None), P(), P(), P())
    out_specs = P(("wide", "narrow"), None)
    body = functools.partial(shards, mesh.shape["wide"], mesh.shape["narrow"])
    return jax.shard_map(body, mesh=mesh, in_specs=in_specs, out_specs=out_specs, check_vma=False)
```

```python
import functools

import jax
import jax.numpy as jnp
from jax import lax
from jax.experimental import pallas as pl
from jax.experimental.pallas import tpu as pltpu
from jax.sharding import PartitionSpec as P

LANES = 128
MIB = 2**20
X, Y, Z1, Z2, Z3 = 1, 2, 4, 8, 12
INNER, OUTER = (1, 2), (0, 3)
LOAD, MULTIPLY, STEP, PICK = "load", "multiply", "step", "pick"
EVENTS = (
    ("A", Z1, "O"), ("C1", Z3, "O", INNER), ("XO", X, "O"), ("YO", Y, "O"), LOAD, ("A",), STEP, ("C1",),
    ("C2", Z3, "O", OUTER), ("YA", Y, "A"), ("YO",), ("DO", X, "YO"), ("XO",), MULTIPLY, ("C2",), (PICK, "C"),
    ("XC", X, "C"), ("B", Z1, "C"), ("YC", Y, "C"), ("YA",), ("DO",), MULTIPLY, ("XC",), ("XB", Z1, "XC"), ("B",),
    ("YB", Y, "B"), ("YC",), ("XA", X, "A"), ("DC", X, "YC"), MULTIPLY, ("XB",), ("DB", Y, "XB"), ("DA", Z1, "DO"),
    ("YB",), ("XA",), MULTIPLY, ("DA",), ("DC",), ("DB",),
)
LOADS = {0: (1, 3), 1: (3, None)}
KEEP_AT = 2
COST = pl.CostEstimate(flops=1, bytes_accessed=4 * 10**6, transcendentals=0)
ANYWHERE = pl.BlockSpec(memory_space=pl.ANY)
VMEM = pl.BlockSpec(memory_space=pltpu.VMEM)


def lookup_irrep(orbitals, table):
    hits = orbitals[..., None] == jnp.arange(table.shape[0], dtype=jnp.int32)
    return jnp.sum(jnp.where(hits, table, 0), axis=-1)


def transpose_kernel(pairs, tile_ref, out_ref, flat, rows):
    depth = flat.shape[0] // 3
    flat[...] = tile_ref[...].astype(jnp.float32).reshape(flat.shape)
    x0, x1, x2 = [flat[pl.ds(s, depth, stride=3), :] for s in range(3)]
    lane = lax.broadcasted_iota(jnp.int32, x0.shape, 1)
    rows[pl.ds(0, depth, stride=4), :] = x0
    rows[pl.ds(1, depth, stride=4), :] = jnp.where(lane < 32, pltpu.roll(x0, 32, 1), pltpu.roll(x1, 32, 1))
    rows[pl.ds(2, depth, stride=4), :] = jnp.where(lane < 64, pltpu.roll(x1, 64, 1), pltpu.roll(x2, 64, 1))
    rows[pl.ds(3, depth, stride=4), :] = pltpu.roll(x2, 96, 1)
    out_ref[...] = rows[...].T[:pairs].astype(out_ref.dtype)


def transposed_tile(tile, pairs):
    size = tile.shape[1]
    return pl.pallas_call(
        functools.partial(transpose_kernel, pairs),
        out_shape=jax.ShapeDtypeStruct((pairs, size // pairs), tile.dtype),
        scratch_shapes=[
            pltpu.VMEM((size // LANES, LANES), jnp.float32),
            pltpu.VMEM((size // pairs, LANES), jnp.float32),
        ],
        compiler_params=pltpu.CompilerParams(vmem_limit_bytes=8 * MIB),
        name="transpose_tile",
    )(tile)


def product(left, right):
    return lax.dot_general(left, right, (((1,), (1,)), ((), ())), preferred_element_type=jnp.float32)


def step_kernel(mark_ref, out_ref):
    pass


def mark_step(mark):
    return pl.pallas_call(
        step_kernel,
        out_shape=jax.ShapeDtypeStruct(mark.shape, mark.dtype),
        in_specs=[ANYWHERE],
        out_specs=ANYWHERE,
        input_output_aliases={0: 0},
        cost_estimate=COST,
        compiler_params=pltpu.CompilerParams(vmem_limit_bytes=MIB),
        name="mark_step",
    )(mark)


def pick_kernel(inner_ref, outer_ref, mark_ref, out_ref, mark_out_ref):
    z = lax.axis_index("wide") // 4
    inner = jnp.logical_and(z > 0, z < 3)

    @pl.when(inner)
    def _():
        out_ref[...] = inner_ref[...]

    @pl.when(jnp.logical_not(inner))
    def _():
        out_ref[...] = outer_ref[...]


def pick_level(inner, outer, mark):
    return pl.pallas_call(
        pick_kernel,
        out_shape=[jax.ShapeDtypeStruct(inner.shape, inner.dtype), jax.ShapeDtypeStruct(mark.shape, mark.dtype)],
        in_specs=[VMEM, VMEM, ANYWHERE],
        out_specs=[VMEM, ANYWHERE],
        input_output_aliases={2: 1},
        cost_estimate=COST,
        compiler_params=pltpu.CompilerParams(vmem_limit_bytes=2 * MIB),
        name="pick_level",
    )(inner, outer, mark)


def keep_of(rows, pairs, pair_count, orbital_table, pair_table):
    columns = jnp.concatenate([orbital_table, orbital_table]).astype(jnp.float32).T
    row_labels = [jnp.zeros((1, rows.shape[1]), jnp.float32) for _ in range(2)]
    for block in range(orbital_table.shape[0]):
        ids = lax.broadcasted_iota(jnp.int32, (LANES, rows.shape[1]), 0) + block * LANES
        for k in range(2):
            hits = jnp.where(ids == rows[k:k + 1], columns[:, block:block + 1], 0.0)
            row_labels[k] += jnp.sum(hits, axis=0, keepdims=True)
    row_sym = jnp.bitwise_xor(*[label.astype(jnp.int32) for label in row_labels]).astype(jnp.float32)
    pair_labels = jnp.zeros(pairs.shape, jnp.int32)
    for k in range(pair_table.shape[0]):
        pair_labels = jnp.where(pairs == k, pair_table[k], pair_labels)
    pair_sym = jnp.bitwise_xor(pair_labels[0:1], pair_labels[1:2]).astype(jnp.float32)
    pair_sym = jnp.concatenate([pair_sym, jnp.zeros((1, -pair_count % LANES), jnp.float32)], axis=1)
    pair_sym = jnp.broadcast_to(pair_sym, (8, pair_sym.shape[1])).T[:pair_count, 0:1]
    return (pair_sym == row_sym).astype(jnp.float32)


def work_kernel(parts, depth, mark_ref, *refs):
    refs = list(refs)
    take = lambda count: [refs.pop(0) for _ in range(count)]
    me = lax.axis_index("wide")
    integrals = take(1) if parts["loads"] else []
    tables = take(4 if parts["pairs"] else 0)
    loaded = take(1 if parts["chunks"] else 0)
    chunks = take(parts["chunks"])
    total = take(parts["total"])
    keeps = take(1 if parts["pairs"] else 0)
    fetched = take(len(parts["loads"]))
    sums_out = take(2 if parts["last"] else 1 if parts["chunks"] else 0)
    copies = []
    for target, distances in zip(fetched, parts["loads"]):
        for k, distance in enumerate(distances):
            column = pl.multiple_of((me ^ distance) * depth, depth)
            source = integrals[0].at[:, pl.ds(column, depth)]
            copies.append(pltpu.make_async_copy(source, target.at[:, pl.ds(k * depth, depth)], refs[-1].at[len(copies)]))
    for copy in copies:
        copy.start()
    if chunks:
        sums = total[0][...] if total else None
        for k, chunk in enumerate(chunks):
            term = product(loaded[0][:, pl.ds(k * depth, depth)], chunk[...])
            sums = term if sums is None else sums + term
        if parts["last"]:
            part = parts["last"]
            mine = pl.multiple_of(lax.axis_index("narrow") * part, part)
            whole = refs.pop()
            whole[...] = sums.T
            sums_out[0][...] = whole[:, pl.ds(mine, part)]
            sums_out[1][...] = whole[:, pl.ds(part - mine, part)]
        else:
            sums_out[0][...] = sums
    if tables:
        part = keeps[0].shape[1]
        rows = tables[0][:, pl.ds(pl.multiple_of(lax.axis_index("narrow") * part, part), part)]
        keeps[0][...] = keep_of(rows, tables[1][...], parts["pairs"], tables[2][...], tables[3])
    for copy in copies:
        copy.wait()


def work(mark, depth, integrals=None, loads=(), loaded=None, chunks=(), total=None, last=0, tables=(), keep_shape=None):
    parts = {
        "loads": loads, "chunks": len(chunks), "total": 0 if total is None else 1, "last": last,
        "pairs": keep_shape[0] if tables else 0,
    }
    operands, specs, outs = [], [], []
    if loads:
        operands.append(integrals)
        specs.append(ANYWHERE)
    if tables:
        operands += tables
        specs += [VMEM, VMEM, VMEM, pl.BlockSpec(memory_space=pltpu.SMEM)]
        outs.append(jax.ShapeDtypeStruct(keep_shape, jnp.float32))
    for distances in loads:
        outs.append(jax.ShapeDtypeStruct((integrals.shape[0], depth * len(distances)), integrals.dtype))
    if chunks:
        operands += [loaded, *chunks] + ([] if total is None else [total])
        specs += [VMEM] * (len(operands) - len(specs))
        rows, pairs = loaded.shape[0], chunks[0].shape[0]
        outs += [jax.ShapeDtypeStruct(shape, jnp.float32) for shape in ([(pairs, last)] * 2 if last else [(rows, pairs)])]
    count = sum(len(distances) for distances in loads)
    *result, mark = pl.pallas_call(
        functools.partial(work_kernel, parts, depth),
        out_shape=outs + [jax.ShapeDtypeStruct(mark.shape, mark.dtype)],
        in_specs=[ANYWHERE] + specs,
        out_specs=[VMEM] * len(outs) + [ANYWHERE],
        input_output_aliases={0: len(outs)},
        scratch_shapes=(
            [pltpu.SemaphoreType.DMA((count,))] if count else [pltpu.VMEM((pairs, rows), jnp.float32)] if last else []
        ),
        cost_estimate=COST,
        compiler_params=pltpu.CompilerParams(vmem_limit_bytes=(20 if not loads else 30 if chunks else 40) * MIB),
        name="work",
    )(mark, *operands)
    keep = result.pop(0) if tables else None
    fetched = [result.pop(0) for _ in loads]
    return mark, fetched, (result if last else result.pop(0) if chunks else total), keep


def ring_kernel(integrals_ref, chunk_ref, out_ref):
    @pl.when(pl.program_id(0) == 0)
    def _():
        out_ref[...] = jnp.zeros_like(out_ref)

    out_ref[...] += product(integrals_ref[...], chunk_ref[0])


def gathered_product(integrals, own, axis_size):
    rows, (pairs, depth) = integrals.shape[0], own.shape
    gathered = lax.all_gather(own, "wide", axis=0)
    return pl.pallas_call(
        ring_kernel,
        out_shape=jax.ShapeDtypeStruct((rows, pairs), jnp.float32),
        grid=(axis_size,),
        in_specs=[
            pl.BlockSpec((rows, depth), lambda i: (0, i)),
            pl.BlockSpec((1, pairs, depth), lambda i: (i, 0, 0)),
        ],
        out_specs=pl.BlockSpec((rows, pairs), lambda i: (0, 0)),
        name="gathered_product",
    )(integrals, gathered)


def plan_of_events():
    distance, groups, arrived = {"O": 0}, [], ["O"]
    for event in EVENTS:
        if event in (LOAD, STEP):
            continue
        if event == MULTIPLY:
            groups.append(arrived)
            arrived = []
        elif event[0] == PICK:
            arrived.append(event[1])
        elif len(event) == 4:
            distance[event[0][:-1]] = distance[event[2]] ^ event[1]
        elif len(event) == 3:
            name, step, source = event
            distance[name] = distance[source] ^ step
        elif event[0] in distance:
            arrived.append(event[0])
    groups.append(arrived)
    assert sorted(distance[name] for names in groups for name in names) == list(range(16))
    return distance, groups


def exchanged_product(integrals, own, tables, keep_shape):
    depth = own.shape[1]
    distance, groups = plan_of_events()
    wanted = [tuple(distance[name] for name in names) for names in groups]
    held, fresh, loaded, total, keep, multiplied = {"O": own}, [], [], None, None, 0
    mark = jnp.zeros((8, LANES), jnp.float32)

    def ready():
        arrived = [held[name] for name in fresh]
        fresh.clear()
        return lax.optimization_barrier((mark, *arrived))[0]

    def multiply(**more):
        chunks = [held[name] for name in groups[multiplied]]
        return work(ready(), depth, loaded=loaded[multiplied], chunks=chunks, total=total, **more)

    for event in EVENTS:
        if event == STEP:
            mark = mark_step(ready())
        elif event == LOAD:
            mark, loaded, *_ = work(ready(), depth, integrals=integrals, loads=tuple(wanted[:1]))
        elif event == MULTIPLY:
            more = {}
            if multiplied in LOADS:
                more = {"integrals": integrals, "loads": tuple(wanted[slice(*LOADS[multiplied])])}
            if multiplied == KEEP_AT:
                more |= {"tables": tables, "keep_shape": keep_shape}
            mark, fetched, total, keeps = multiply(**more)
            loaded = loaded + fetched
            keep = keep if keeps is None else keeps
            multiplied += 1
        elif event[0] == PICK:
            name = event[1]
            held[name], mark = pick_level(held[name + "1"], held[name + "2"], ready())
        elif len(event) >= 3:
            name, step, source = event[:3]
            levels = event[3] if len(event) == 4 else range(4)
            value, mark, *_ = lax.optimization_barrier((held[source], mark, *[held[n] for n in fresh]))
            held[name] = lax.ppermute(value, "wide", [(i, i ^ step) for i in range(16) if i // 4 in levels])
        else:
            fresh.append(event[0])
    return *multiply(last=keep_shape[1])[2], keep


def masked_block(integrals, own, wide, row_orbitals, orb_irrep, occ_pairs, occ_irrep):
    row_labels = lookup_irrep(row_orbitals, orb_irrep)
    pair_labels = lookup_irrep(occ_pairs, occ_irrep)
    row_sym = jnp.bitwise_xor(row_labels[:, 0], row_labels[:, 1])
    pair_sym = jnp.bitwise_xor(pair_labels[:, 0], pair_labels[:, 1])
    block = gathered_product(integrals, own, wide)
    return jnp.where(row_sym[:, None] == pair_sym[None, :], block, jnp.zeros_like(block))


def shards(wide, narrow, integrals, amp_tiles, row_orbitals, orb_irrep, occ_pairs, occ_irrep):
    pairs = occ_pairs.shape[0]
    part = integrals.shape[0] // narrow
    own = transposed_tile(amp_tiles, pairs)
    if (wide, narrow) != (16, 2):
        block = masked_block(integrals, own, wide, row_orbitals, orb_irrep, occ_pairs, occ_irrep)
        return lax.psum_scatter(block, "narrow", scatter_dimension=0, tiled=True)
    tables = (row_orbitals.T, occ_pairs.T, orb_irrep.reshape(-1, LANES), occ_irrep)
    mine, other, keep = exchanged_product(integrals, own, tables, (pairs, part))
    summed = mine + lax.ppermute(other, "narrow", [(0, 1), (1, 0)])
    return jnp.where(keep > 0, summed, jnp.zeros_like(summed)).T


def solution(mesh):
    in_specs = (P("wide", "narrow"), P("narrow", "wide"), P("wide", None), P(), P(), P())
    out_specs = P(("wide", "narrow"), None)
    body = functools.partial(shards, mesh.shape["wide"], mesh.shape["narrow"])
    return jax.shard_map(body, mesh=mesh, in_specs=in_specs, out_specs=out_specs, check_vma=False)
```

```python
import functools

import jax
import jax.numpy as jnp
from jax import lax
from jax.experimental import pallas as pl
from jax.experimental.pallas import tpu as pltpu
from jax.sharding import PartitionSpec as P

LANES = 128
MIB = 2**20
X, Y, Z1, Z2, Z3 = 1, 2, 4, 8, 12
INNER, OUTER = (1, 2), (0, 3)
LOAD, MULTIPLY, STEP, PICK = "load", "multiply", "step", "pick"
EVENTS = (
    ("A", Z1, "O"), ("C1", Z3, "O", INNER), ("XO", X, "O"), ("YO", Y, "O"), LOAD, ("A",), STEP, ("C1",),
    ("C2", Z3, "O", OUTER), ("YA", Y, "A"), ("YO",), ("DO", X, "YO"), ("XO",), MULTIPLY, ("C2",), (PICK, "C"),
    ("XC", X, "C"), ("B", Z1, "C"), ("YC", Y, "C"), ("YA",), ("DO",), MULTIPLY, ("XC",), ("XB", Z1, "XC"), ("B",),
    ("YB", Y, "B"), ("YC",), ("XA", X, "A"), ("DC", X, "YC"), MULTIPLY, ("XB",), ("DB", Y, "XB"), ("DA", Z1, "DO"),
    ("YB",), ("XA",), MULTIPLY, ("DC",), ("DA",), MULTIPLY, ("DB",),
)
LOADS = {0: (1, 3), 1: (3, None)}
KEEP_AT = 2
COST = pl.CostEstimate(flops=1, bytes_accessed=4 * 10**6, transcendentals=0)
ANYWHERE = pl.BlockSpec(memory_space=pl.ANY)
VMEM = pl.BlockSpec(memory_space=pltpu.VMEM)


def lookup_irrep(orbitals, table):
    hits = orbitals[..., None] == jnp.arange(table.shape[0], dtype=jnp.int32)
    return jnp.sum(jnp.where(hits, table, 0), axis=-1)


def transpose_kernel(pairs, tile_ref, out_ref, flat, rows):
    depth = flat.shape[0] // 3
    flat[...] = tile_ref[...].astype(jnp.float32).reshape(flat.shape)
    x0, x1, x2 = [flat[pl.ds(s, depth, stride=3), :] for s in range(3)]
    lane = lax.broadcasted_iota(jnp.int32, x0.shape, 1)
    rows[pl.ds(0, depth, stride=4), :] = x0
    rows[pl.ds(1, depth, stride=4), :] = jnp.where(lane < 32, pltpu.roll(x0, 32, 1), pltpu.roll(x1, 32, 1))
    rows[pl.ds(2, depth, stride=4), :] = jnp.where(lane < 64, pltpu.roll(x1, 64, 1), pltpu.roll(x2, 64, 1))
    rows[pl.ds(3, depth, stride=4), :] = pltpu.roll(x2, 96, 1)
    out_ref[...] = rows[...].T[:pairs].astype(out_ref.dtype)


def transposed_tile(tile, pairs):
    size = tile.shape[1]
    return pl.pallas_call(
        functools.partial(transpose_kernel, pairs),
        out_shape=jax.ShapeDtypeStruct((pairs, size // pairs), tile.dtype),
        scratch_shapes=[
            pltpu.VMEM((size // LANES, LANES), jnp.float32),
            pltpu.VMEM((size // pairs, LANES), jnp.float32),
        ],
        compiler_params=pltpu.CompilerParams(vmem_limit_bytes=8 * MIB),
        name="transpose_tile",
    )(tile)


def product(left, right):
    return lax.dot_general(left, right, (((1,), (1,)), ((), ())), preferred_element_type=jnp.float32)


def step_kernel(mark_ref, out_ref):
    pass


def mark_step(mark):
    return pl.pallas_call(
        step_kernel,
        out_shape=jax.ShapeDtypeStruct(mark.shape, mark.dtype),
        in_specs=[ANYWHERE],
        out_specs=ANYWHERE,
        input_output_aliases={0: 0},
        cost_estimate=COST,
        compiler_params=pltpu.CompilerParams(vmem_limit_bytes=MIB),
        name="mark_step",
    )(mark)


def pick_kernel(inner_ref, outer_ref, mark_ref, out_ref, mark_out_ref):
    z = lax.axis_index("wide") // 4
    inner = jnp.logical_and(z > 0, z < 3)

    @pl.when(inner)
    def _():
        out_ref[...] = inner_ref[...]

    @pl.when(jnp.logical_not(inner))
    def _():
        out_ref[...] = outer_ref[...]


def pick_level(inner, outer, mark):
    return pl.pallas_call(
        pick_kernel,
        out_shape=[jax.ShapeDtypeStruct(inner.shape, inner.dtype), jax.ShapeDtypeStruct(mark.shape, mark.dtype)],
        in_specs=[VMEM, VMEM, ANYWHERE],
        out_specs=[VMEM, ANYWHERE],
        input_output_aliases={2: 1},
        cost_estimate=COST,
        compiler_params=pltpu.CompilerParams(vmem_limit_bytes=2 * MIB),
        name="pick_level",
    )(inner, outer, mark)


def keep_of(rows, pairs, pair_count, orbital_table, pair_table):
    columns = jnp.concatenate([orbital_table, orbital_table]).astype(jnp.float32).T
    row_labels = [jnp.zeros((1, rows.shape[1]), jnp.float32) for _ in range(2)]
    for block in range(orbital_table.shape[0]):
        ids = lax.broadcasted_iota(jnp.int32, (LANES, rows.shape[1]), 0) + block * LANES
        for k in range(2):
            hits = jnp.where(ids == rows[k:k + 1], columns[:, block:block + 1], 0.0)
            row_labels[k] += jnp.sum(hits, axis=0, keepdims=True)
    row_sym = jnp.bitwise_xor(*[label.astype(jnp.int32) for label in row_labels]).astype(jnp.float32)
    pair_labels = jnp.zeros(pairs.shape, jnp.int32)
    for k in range(pair_table.shape[0]):
        pair_labels = jnp.where(pairs == k, pair_table[k], pair_labels)
    pair_sym = jnp.bitwise_xor(pair_labels[0:1], pair_labels[1:2]).astype(jnp.float32)
    pair_sym = jnp.concatenate([pair_sym, jnp.zeros((1, -pair_count % LANES), jnp.float32)], axis=1)
    pair_sym = jnp.broadcast_to(pair_sym, (8, pair_sym.shape[1])).T[:pair_count, 0:1]
    return (pair_sym == row_sym).astype(jnp.float32)


def work_kernel(parts, depth, mark_ref, *refs):
    refs = list(refs)
    take = lambda count: [refs.pop(0) for _ in range(count)]
    me = lax.axis_index("wide")
    integrals = take(1) if parts["loads"] else []
    tables = take(4 if parts["pairs"] else 0)
    loaded = take(1 if parts["chunks"] else 0)
    chunks = take(parts["chunks"])
    total = take(parts["total"])
    keeps = take(1 if parts["pairs"] else 0)
    fetched = take(len(parts["loads"]))
    sums_out = take(2 if parts["last"] else 1 if parts["chunks"] else 0)
    copies = []
    for target, distances in zip(fetched, parts["loads"]):
        for k, distance in enumerate(distances):
            column = pl.multiple_of((me ^ distance) * depth, depth)
            source = integrals[0].at[:, pl.ds(column, depth)]
            copies.append(pltpu.make_async_copy(source, target.at[:, pl.ds(k * depth, depth)], refs[-1].at[len(copies)]))
    for copy in copies:
        copy.start()
    if chunks:
        sums = total[0][...] if total else None
        for k, chunk in enumerate(chunks):
            term = product(loaded[0][:, pl.ds(k * depth, depth)], chunk[...])
            sums = term if sums is None else sums + term
        if parts["last"]:
            part = parts["last"]
            mine = pl.multiple_of(lax.axis_index("narrow") * part, part)
            whole = refs.pop()
            whole[...] = sums.T
            sums_out[0][...] = whole[:, pl.ds(mine, part)]
            sums_out[1][...] = whole[:, pl.ds(part - mine, part)]
        else:
            sums_out[0][...] = sums
    if tables:
        part = keeps[0].shape[1]
        rows = tables[0][:, pl.ds(pl.multiple_of(lax.axis_index("narrow") * part, part), part)]
        keeps[0][...] = keep_of(rows, tables[1][...], parts["pairs"], tables[2][...], tables[3])
    for copy in copies:
        copy.wait()


def work(mark, depth, integrals=None, loads=(), loaded=None, chunks=(), total=None, last=0, tables=(), keep_shape=None):
    parts = {
        "loads": loads, "chunks": len(chunks), "total": 0 if total is None else 1, "last": last,
        "pairs": keep_shape[0] if tables else 0,
    }
    operands, specs, outs = [], [], []
    if loads:
        operands.append(integrals)
        specs.append(ANYWHERE)
    if tables:
        operands += tables
        specs += [VMEM, VMEM, VMEM, pl.BlockSpec(memory_space=pltpu.SMEM)]
        outs.append(jax.ShapeDtypeStruct(keep_shape, jnp.float32))
    for distances in loads:
        outs.append(jax.ShapeDtypeStruct((integrals.shape[0], depth * len(distances)), integrals.dtype))
    if chunks:
        operands += [loaded, *chunks] + ([] if total is None else [total])
        specs += [VMEM] * (len(operands) - len(specs))
        rows, pairs = loaded.shape[0], chunks[0].shape[0]
        outs += [jax.ShapeDtypeStruct(shape, jnp.float32) for shape in ([(pairs, last)] * 2 if last else [(rows, pairs)])]
    count = sum(len(distances) for distances in loads)
    *result, mark = pl.pallas_call(
        functools.partial(work_kernel, parts, depth),
        out_shape=outs + [jax.ShapeDtypeStruct(mark.shape, mark.dtype)],
        in_specs=[ANYWHERE] + specs,
        out_specs=[VMEM] * len(outs) + [ANYWHERE],
        input_output_aliases={0: len(outs)},
        scratch_shapes=(
            [pltpu.SemaphoreType.DMA((count,))] if count else [pltpu.VMEM((pairs, rows), jnp.float32)] if last else []
        ),
        cost_estimate=COST,
        compiler_params=pltpu.CompilerParams(vmem_limit_bytes=(20 if not loads else 30 if chunks else 40) * MIB),
        name="work",
    )(mark, *operands)
    keep = result.pop(0) if tables else None
    fetched = [result.pop(0) for _ in loads]
    return mark, fetched, (result if last else result.pop(0) if chunks else total), keep


def ring_kernel(integrals_ref, chunk_ref, out_ref):
    @pl.when(pl.program_id(0) == 0)
    def _():
        out_ref[...] = jnp.zeros_like(out_ref)

    out_ref[...] += product(integrals_ref[...], chunk_ref[0])


def gathered_product(integrals, own, axis_size):
    rows, (pairs, depth) = integrals.shape[0], own.shape
    gathered = lax.all_gather(own, "wide", axis=0)
    return pl.pallas_call(
        ring_kernel,
        out_shape=jax.ShapeDtypeStruct((rows, pairs), jnp.float32),
        grid=(axis_size,),
        in_specs=[
            pl.BlockSpec((rows, depth), lambda i: (0, i)),
            pl.BlockSpec((1, pairs, depth), lambda i: (i, 0, 0)),
        ],
        out_specs=pl.BlockSpec((rows, pairs), lambda i: (0, 0)),
        name="gathered_product",
    )(integrals, gathered)


def plan_of_events():
    distance, groups, arrived = {"O": 0}, [], ["O"]
    for event in EVENTS:
        if event in (LOAD, STEP):
            continue
        if event == MULTIPLY:
            groups.append(arrived)
            arrived = []
        elif event[0] == PICK:
            arrived.append(event[1])
        elif len(event) == 4:
            distance[event[0][:-1]] = distance[event[2]] ^ event[1]
        elif len(event) == 3:
            name, step, source = event
            distance[name] = distance[source] ^ step
        elif event[0] in distance:
            arrived.append(event[0])
    groups.append(arrived)
    assert sorted(distance[name] for names in groups for name in names) == list(range(16))
    return distance, groups


def exchanged_product(integrals, own, tables, keep_shape):
    depth = own.shape[1]
    distance, groups = plan_of_events()
    wanted = [tuple(distance[name] for name in names) for names in groups]
    held, fresh, loaded, total, keep, multiplied = {"O": own}, [], [], None, None, 0
    mark = jnp.zeros((8, LANES), jnp.float32)

    def ready():
        arrived = [held[name] for name in fresh]
        fresh.clear()
        return lax.optimization_barrier((mark, *arrived))[0]

    def multiply(**more):
        chunks = [held[name] for name in groups[multiplied]]
        return work(ready(), depth, loaded=loaded[multiplied], chunks=chunks, total=total, **more)

    for event in EVENTS:
        if event == STEP:
            mark = mark_step(ready())
        elif event == LOAD:
            mark, loaded, *_ = work(ready(), depth, integrals=integrals, loads=tuple(wanted[:1]))
        elif event == MULTIPLY:
            more = {}
            if multiplied in LOADS:
                more = {"integrals": integrals, "loads": tuple(wanted[slice(*LOADS[multiplied])])}
            if multiplied == KEEP_AT:
                more |= {"tables": tables, "keep_shape": keep_shape}
            mark, fetched, total, keeps = multiply(**more)
            loaded = loaded + fetched
            keep = keep if keeps is None else keeps
            multiplied += 1
        elif event[0] == PICK:
            name = event[1]
            held[name], mark = pick_level(held[name + "1"], held[name + "2"], ready())
        elif len(event) >= 3:
            name, step, source = event[:3]
            levels = event[3] if len(event) == 4 else range(4)
            value, mark, *_ = lax.optimization_barrier((held[source], mark, *[held[n] for n in fresh]))
            held[name] = lax.ppermute(value, "wide", [(i, i ^ step) for i in range(16) if i // 4 in levels])
        else:
            fresh.append(event[0])
    return *multiply(last=keep_shape[1])[2], keep


def masked_block(integrals, own, wide, row_orbitals, orb_irrep, occ_pairs, occ_irrep):
    row_labels = lookup_irrep(row_orbitals, orb_irrep)
    pair_labels = lookup_irrep(occ_pairs, occ_irrep)
    row_sym = jnp.bitwise_xor(row_labels[:, 0], row_labels[:, 1])
    pair_sym = jnp.bitwise_xor(pair_labels[:, 0], pair_labels[:, 1])
    block = gathered_product(integrals, own, wide)
    return jnp.where(row_sym[:, None] == pair_sym[None, :], block, jnp.zeros_like(block))


def shards(wide, narrow, integrals, amp_tiles, row_orbitals, orb_irrep, occ_pairs, occ_irrep):
    pairs = occ_pairs.shape[0]
    part = integrals.shape[0] // narrow
    own = transposed_tile(amp_tiles, pairs)
    if (wide, narrow) != (16, 2):
        block = masked_block(integrals, own, wide, row_orbitals, orb_irrep, occ_pairs, occ_irrep)
        return lax.psum_scatter(block, "narrow", scatter_dimension=0, tiled=True)
    tables = (row_orbitals.T, occ_pairs.T, orb_irrep.reshape(-1, LANES), occ_irrep)
    mine, other, keep = exchanged_product(integrals, own, tables, (pairs, part))
    summed = mine + lax.ppermute(other, "narrow", [(0, 1), (1, 0)])
    return jnp.where(keep > 0, summed, jnp.zeros_like(summed)).T


def solution(mesh):
    in_specs = (P("wide", "narrow"), P("narrow", "wide"), P("wide", None), P(), P(), P())
    out_specs = P(("wide", "narrow"), None)
    body = functools.partial(shards, mesh.shape["wide"], mesh.shape["narrow"])
    return jax.shard_map(body, mesh=mesh, in_specs=in_specs, out_specs=out_specs, check_vma=False)
```

```python
import functools

import jax
import jax.numpy as jnp
from jax import lax
from jax.experimental import pallas as pl
from jax.experimental.pallas import tpu as pltpu
from jax.sharding import PartitionSpec as P

LANES = 128
MIB = 2**20
X, Y, Z1, Z2, Z3 = 1, 2, 4, 8, 12
INNER, OUTER = (1, 2), (0, 3)
LOAD, MULTIPLY, STEP, PICK = "load", "multiply", "step", "pick"
EVENTS = (
    ("A", Z1, "O"), ("C1", Z3, "O", INNER), ("XO", X, "O"), ("YO", Y, "O"), LOAD, ("A",), STEP, ("C1",),
    ("C2", Z3, "O", OUTER), ("YA", Y, "A"), ("YO",), ("DO", X, "YO"), ("XO",), MULTIPLY, ("C2",), (PICK, "C"),
    ("XC", X, "C"), ("B", Z1, "C"), ("YC", Y, "C"), ("YA",), ("DO",), MULTIPLY, ("XC",), ("XB", Z1, "XC"), ("B",),
    ("YB", Y, "B"), ("YC",), ("XA", X, "A"), ("DC", X, "YC"), MULTIPLY, ("XB",), ("DB", Y, "XB"), ("DA", Z1, "DO"),
    ("YB",), STEP, ("XA",), MULTIPLY, ("DB",), ("DA",), MULTIPLY, ("DC",),
)
LOADS = {0: (1, 3), 1: (3, None)}
KEEP_AT = 2
COST = pl.CostEstimate(flops=1, bytes_accessed=4 * 10**6, transcendentals=0)
ANYWHERE = pl.BlockSpec(memory_space=pl.ANY)
VMEM = pl.BlockSpec(memory_space=pltpu.VMEM)


def lookup_irrep(orbitals, table):
    hits = orbitals[..., None] == jnp.arange(table.shape[0], dtype=jnp.int32)
    return jnp.sum(jnp.where(hits, table, 0), axis=-1)


def transpose_kernel(pairs, tile_ref, out_ref, flat, rows):
    depth = flat.shape[0] // 3
    flat[...] = tile_ref[...].astype(jnp.float32).reshape(flat.shape)
    x0, x1, x2 = [flat[pl.ds(s, depth, stride=3), :] for s in range(3)]
    lane = lax.broadcasted_iota(jnp.int32, x0.shape, 1)
    rows[pl.ds(0, depth, stride=4), :] = x0
    rows[pl.ds(1, depth, stride=4), :] = jnp.where(lane < 32, pltpu.roll(x0, 32, 1), pltpu.roll(x1, 32, 1))
    rows[pl.ds(2, depth, stride=4), :] = jnp.where(lane < 64, pltpu.roll(x1, 64, 1), pltpu.roll(x2, 64, 1))
    rows[pl.ds(3, depth, stride=4), :] = pltpu.roll(x2, 96, 1)
    out_ref[...] = rows[...].T[:pairs].astype(out_ref.dtype)


def transposed_tile(tile, pairs):
    size = tile.shape[1]
    return pl.pallas_call(
        functools.partial(transpose_kernel, pairs),
        out_shape=jax.ShapeDtypeStruct((pairs, size // pairs), tile.dtype),
        scratch_shapes=[
            pltpu.VMEM((size // LANES, LANES), jnp.float32),
            pltpu.VMEM((size // pairs, LANES), jnp.float32),
        ],
        compiler_params=pltpu.CompilerParams(vmem_limit_bytes=8 * MIB),
        name="transpose_tile",
    )(tile)


def product(left, right):
    return lax.dot_general(left, right, (((1,), (1,)), ((), ())), preferred_element_type=jnp.float32)


def step_kernel(mark_ref, out_ref):
    pass


def mark_step(mark):
    return pl.pallas_call(
        step_kernel,
        out_shape=jax.ShapeDtypeStruct(mark.shape, mark.dtype),
        in_specs=[ANYWHERE],
        out_specs=ANYWHERE,
        input_output_aliases={0: 0},
        cost_estimate=COST,
        compiler_params=pltpu.CompilerParams(vmem_limit_bytes=MIB),
        name="mark_step",
    )(mark)


def pick_kernel(inner_ref, outer_ref, mark_ref, out_ref, mark_out_ref):
    z = lax.axis_index("wide") // 4
    inner = jnp.logical_and(z > 0, z < 3)

    @pl.when(inner)
    def _():
        out_ref[...] = inner_ref[...]

    @pl.when(jnp.logical_not(inner))
    def _():
        out_ref[...] = outer_ref[...]


def pick_level(inner, outer, mark):
    return pl.pallas_call(
        pick_kernel,
        out_shape=[jax.ShapeDtypeStruct(inner.shape, inner.dtype), jax.ShapeDtypeStruct(mark.shape, mark.dtype)],
        in_specs=[VMEM, VMEM, ANYWHERE],
        out_specs=[VMEM, ANYWHERE],
        input_output_aliases={2: 1},
        cost_estimate=COST,
        compiler_params=pltpu.CompilerParams(vmem_limit_bytes=2 * MIB),
        name="pick_level",
    )(inner, outer, mark)


def keep_of(rows, pairs, pair_count, orbital_table, pair_table):
    columns = jnp.concatenate([orbital_table, orbital_table]).astype(jnp.float32).T
    row_labels = [jnp.zeros((1, rows.shape[1]), jnp.float32) for _ in range(2)]
    for block in range(orbital_table.shape[0]):
        ids = lax.broadcasted_iota(jnp.int32, (LANES, rows.shape[1]), 0) + block * LANES
        for k in range(2):
            hits = jnp.where(ids == rows[k:k + 1], columns[:, block:block + 1], 0.0)
            row_labels[k] += jnp.sum(hits, axis=0, keepdims=True)
    row_sym = jnp.bitwise_xor(*[label.astype(jnp.int32) for label in row_labels]).astype(jnp.float32)
    pair_labels = jnp.zeros(pairs.shape, jnp.int32)
    for k in range(pair_table.shape[0]):
        pair_labels = jnp.where(pairs == k, pair_table[k], pair_labels)
    pair_sym = jnp.bitwise_xor(pair_labels[0:1], pair_labels[1:2]).astype(jnp.float32)
    pair_sym = jnp.concatenate([pair_sym, jnp.zeros((1, -pair_count % LANES), jnp.float32)], axis=1)
    pair_sym = jnp.broadcast_to(pair_sym, (8, pair_sym.shape[1])).T[:pair_count, 0:1]
    return (pair_sym == row_sym).astype(jnp.float32)


def work_kernel(parts, depth, mark_ref, *refs):
    refs = list(refs)
    take = lambda count: [refs.pop(0) for _ in range(count)]
    me = lax.axis_index("wide")
    integrals = take(1) if parts["loads"] else []
    tables = take(4 if parts["pairs"] else 0)
    loaded = take(1 if parts["chunks"] else 0)
    chunks = take(parts["chunks"])
    total = take(parts["total"])
    keeps = take(1 if parts["pairs"] else 0)
    fetched = take(len(parts["loads"]))
    sums_out = take(2 if parts["last"] else 1 if parts["chunks"] else 0)
    copies = []
    for target, distances in zip(fetched, parts["loads"]):
        for k, distance in enumerate(distances):
            column = pl.multiple_of((me ^ distance) * depth, depth)
            source = integrals[0].at[:, pl.ds(column, depth)]
            copies.append(pltpu.make_async_copy(source, target.at[:, pl.ds(k * depth, depth)], refs[-1].at[len(copies)]))
    for copy in copies:
        copy.start()
    if chunks:
        sums = total[0][...] if total else None
        for k, chunk in enumerate(chunks):
            term = product(loaded[0][:, pl.ds(k * depth, depth)], chunk[...])
            sums = term if sums is None else sums + term
        if parts["last"]:
            part = parts["last"]
            mine = pl.multiple_of(lax.axis_index("narrow") * part, part)
            whole = refs.pop()
            whole[...] = sums.T
            sums_out[0][...] = whole[:, pl.ds(mine, part)]
            sums_out[1][...] = whole[:, pl.ds(part - mine, part)]
        else:
            sums_out[0][...] = sums
    if tables:
        part = keeps[0].shape[1]
        rows = tables[0][:, pl.ds(pl.multiple_of(lax.axis_index("narrow") * part, part), part)]
        keeps[0][...] = keep_of(rows, tables[1][...], parts["pairs"], tables[2][...], tables[3])
    for copy in copies:
        copy.wait()


def work(mark, depth, integrals=None, loads=(), loaded=None, chunks=(), total=None, last=0, tables=(), keep_shape=None):
    parts = {
        "loads": loads, "chunks": len(chunks), "total": 0 if total is None else 1, "last": last,
        "pairs": keep_shape[0] if tables else 0,
    }
    operands, specs, outs = [], [], []
    if loads:
        operands.append(integrals)
        specs.append(ANYWHERE)
    if tables:
        operands += tables
        specs += [VMEM, VMEM, VMEM, pl.BlockSpec(memory_space=pltpu.SMEM)]
        outs.append(jax.ShapeDtypeStruct(keep_shape, jnp.float32))
    for distances in loads:
        outs.append(jax.ShapeDtypeStruct((integrals.shape[0], depth * len(distances)), integrals.dtype))
    if chunks:
        operands += [loaded, *chunks] + ([] if total is None else [total])
        specs += [VMEM] * (len(operands) - len(specs))
        rows, pairs = loaded.shape[0], chunks[0].shape[0]
        outs += [jax.ShapeDtypeStruct(shape, jnp.float32) for shape in ([(pairs, last)] * 2 if last else [(rows, pairs)])]
    count = sum(len(distances) for distances in loads)
    *result, mark = pl.pallas_call(
        functools.partial(work_kernel, parts, depth),
        out_shape=outs + [jax.ShapeDtypeStruct(mark.shape, mark.dtype)],
        in_specs=[ANYWHERE] + specs,
        out_specs=[VMEM] * len(outs) + [ANYWHERE],
        input_output_aliases={0: len(outs)},
        scratch_shapes=(
            [pltpu.SemaphoreType.DMA((count,))] if count else [pltpu.VMEM((pairs, rows), jnp.float32)] if last else []
        ),
        cost_estimate=COST,
        compiler_params=pltpu.CompilerParams(vmem_limit_bytes=(20 if not loads else 30 if chunks else 40) * MIB),
        name="work",
    )(mark, *operands)
    keep = result.pop(0) if tables else None
    fetched = [result.pop(0) for _ in loads]
    return mark, fetched, (result if last else result.pop(0) if chunks else total), keep


def ring_kernel(integrals_ref, chunk_ref, out_ref):
    @pl.when(pl.program_id(0) == 0)
    def _():
        out_ref[...] = jnp.zeros_like(out_ref)

    out_ref[...] += product(integrals_ref[...], chunk_ref[0])


def gathered_product(integrals, own, axis_size):
    rows, (pairs, depth) = integrals.shape[0], own.shape
    gathered = lax.all_gather(own, "wide", axis=0)
    return pl.pallas_call(
        ring_kernel,
        out_shape=jax.ShapeDtypeStruct((rows, pairs), jnp.float32),
        grid=(axis_size,),
        in_specs=[
            pl.BlockSpec((rows, depth), lambda i: (0, i)),
            pl.BlockSpec((1, pairs, depth), lambda i: (i, 0, 0)),
        ],
        out_specs=pl.BlockSpec((rows, pairs), lambda i: (0, 0)),
        name="gathered_product",
    )(integrals, gathered)


def plan_of_events():
    distance, groups, arrived = {"O": 0}, [], ["O"]
    for event in EVENTS:
        if event in (LOAD, STEP):
            continue
        if event == MULTIPLY:
            groups.append(arrived)
            arrived = []
        elif event[0] == PICK:
            arrived.append(event[1])
        elif len(event) == 4:
            distance[event[0][:-1]] = distance[event[2]] ^ event[1]
        elif len(event) == 3:
            name, step, source = event
            distance[name] = distance[source] ^ step
        elif event[0] in distance:
            arrived.append(event[0])
    groups.append(arrived)
    assert sorted(distance[name] for names in groups for name in names) == list(range(16))
    return distance, groups


def exchanged_product(integrals, own, tables, keep_shape):
    depth = own.shape[1]
    distance, groups = plan_of_events()
    wanted = [tuple(distance[name] for name in names) for names in groups]
    held, fresh, loaded, total, keep, multiplied = {"O": own}, [], [], None, None, 0
    mark = jnp.zeros((8, LANES), jnp.float32)

    def ready():
        arrived = [held[name] for name in fresh]
        fresh.clear()
        return lax.optimization_barrier((mark, *arrived))[0]

    def multiply(**more):
        chunks = [held[name] for name in groups[multiplied]]
        return work(ready(), depth, loaded=loaded[multiplied], chunks=chunks, total=total, **more)

    for event in EVENTS:
        if event == STEP:
            mark = mark_step(ready())
        elif event == LOAD:
            mark, loaded, *_ = work(ready(), depth, integrals=integrals, loads=tuple(wanted[:1]))
        elif event == MULTIPLY:
            more = {}
            if multiplied in LOADS:
                more = {"integrals": integrals, "loads": tuple(wanted[slice(*LOADS[multiplied])])}
            if multiplied == KEEP_AT:
                more |= {"tables": tables, "keep_shape": keep_shape}
            mark, fetched, total, keeps = multiply(**more)
            loaded = loaded + fetched
            keep = keep if keeps is None else keeps
            multiplied += 1
        elif event[0] == PICK:
            name = event[1]
            held[name], mark = pick_level(held[name + "1"], held[name + "2"], ready())
        elif len(event) >= 3:
            name, step, source = event[:3]
            levels = event[3] if len(event) == 4 else range(4)
            value, mark, *_ = lax.optimization_barrier((held[source], mark, *[held[n] for n in fresh]))
            held[name] = lax.ppermute(value, "wide", [(i, i ^ step) for i in range(16) if i // 4 in levels])
        else:
            fresh.append(event[0])
    return *multiply(last=keep_shape[1])[2], keep


def masked_block(integrals, own, wide, row_orbitals, orb_irrep, occ_pairs, occ_irrep):
    row_labels = lookup_irrep(row_orbitals, orb_irrep)
    pair_labels = lookup_irrep(occ_pairs, occ_irrep)
    row_sym = jnp.bitwise_xor(row_labels[:, 0], row_labels[:, 1])
    pair_sym = jnp.bitwise_xor(pair_labels[:, 0], pair_labels[:, 1])
    block = gathered_product(integrals, own, wide)
    return jnp.where(row_sym[:, None] == pair_sym[None, :], block, jnp.zeros_like(block))


def shards(wide, narrow, integrals, amp_tiles, row_orbitals, orb_irrep, occ_pairs, occ_irrep):
    pairs = occ_pairs.shape[0]
    part = integrals.shape[0] // narrow
    own = transposed_tile(amp_tiles, pairs)
    if (wide, narrow) != (16, 2):
        block = masked_block(integrals, own, wide, row_orbitals, orb_irrep, occ_pairs, occ_irrep)
        return lax.psum_scatter(block, "narrow", scatter_dimension=0, tiled=True)
    tables = (row_orbitals.T, occ_pairs.T, orb_irrep.reshape(-1, LANES), occ_irrep)
    mine, other, keep = exchanged_product(integrals, own, tables, (pairs, part))
    summed = mine + lax.ppermute(other, "narrow", [(0, 1), (1, 0)])
    return jnp.where(keep > 0, summed, jnp.zeros_like(summed)).T


def solution(mesh):
    in_specs = (P("wide", "narrow"), P("narrow", "wide"), P("wide", None), P(), P(), P())
    out_specs = P(("wide", "narrow"), None)
    body = functools.partial(shards, mesh.shape["wide"], mesh.shape["narrow"])
    return jax.shard_map(body, mesh=mesh, in_specs=in_specs, out_specs=out_specs, check_vma=False)
```
